32 devices in a mesh: grp: 4 (over x, core), dev: 8 (over z, y).
Axes of the slice: x: 2, y: 2, z: 4, core: 2. Of those that a mesh axis runs over, the one named last changes fastest.
Arguments:
- ctx_hidden: bfloat16 [512, 3584], P('dev'), may hold values from -410 to 410
- step_hidden: bfloat16 [96, 64, 3584], P(('grp', 'dev')), may hold values from -410 to 410
- norm_gain: float32 [3584], replicated, may hold values from 0.1 to 1.9
- w_query: bfloat16 [3584, 1792], P('dev'), may hold values from -4 to 4
- w_keyval: bfloat16 [3584, 512], P('dev'), may hold values from -24 to 24
- step_lengths: int32 [96], P(('grp', 'dev')), may hold values from 1 to 64, as said below
- step_mask: int32 [96, 64, 64], P(('grp', 'dev')), may hold values 0 or 1
Outputs:
- attn_out: bfloat16 [96, 64, 1792], P(('grp', 'dev'))
The draws below stay inside these ranges and needn't reach their ends.
Inputs may be any that keep to these rules, and one draw needn't show every extreme that they name: `step_lengths`: each step's live tokens stand at its front; some solution fills all 64 slots.
All inputs are finite; a program needn't handle non-finite values. No bound on the sum of `step_mask` on one device may be relied on, other than what follows from the above.
Results may differ from the reference program's by a relative error of at most 0.009.
The reference program's roundings to bfloat16 on the way count: a program that leaves them out, or rounds other values in their place, can miss the bound.
Values may be sent and summed in bfloat16 or wider, within the bound.
A program may use at most 128 MiB of HBM per device.

```python
import math
import jax
import jax.numpy as jnp
from jax import lax

MODEL_WIDTH = 3584
QUERY_HEADS = 14
KEYVAL_HEADS = 2
HEAD_SIZE = 128
STEP_SLOTS = 64
SAMPLES = 96
CONTEXT_TOKENS = 512


def with_scales(key, plain_rows):
    key_rows, key_cols = jax.random.split(key)
    row_scale = jnp.exp(jax.random.uniform(key_rows, (plain_rows.shape[0], 1), jnp.float32) * math.log(10.0))
    col_scale = jnp.exp(jax.random.uniform(key_cols, (1, MODEL_WIDTH), jnp.float32) * math.log(10.0))
    return plain_rows * row_scale * col_scale


def draw_ctx_hidden(key, part):
    key = jax.random.fold_in(key, 1)
    key_drawn, key_scale = jax.random.split(key)
    plain_rows = jax.random.truncated_normal(key_drawn, -4.0, 4.0, (CONTEXT_TOKENS, MODEL_WIDTH), jnp.float32)
    return with_scales(key_scale, plain_rows).astype(jnp.bfloat16)


def draw_step_hidden(key, part):
    key = jax.random.fold_in(key, 2)
    key_drawn, key_scale = jax.random.split(key)
    plain_rows = jax.random.truncated_normal(key_drawn, -4.0, 4.0, (SAMPLES * STEP_SLOTS, MODEL_WIDTH), jnp.float32)
    drawn_rows = with_scales(key_scale, plain_rows).reshape(SAMPLES, STEP_SLOTS, MODEL_WIDTH)
    return drawn_rows.astype(jnp.bfloat16)


def draw_w_query(key, part):
    key = jax.random.fold_in(key, 3)
    score_matrix = jax.random.truncated_normal(key, -4.0, 4.0, (MODEL_WIDTH, QUERY_HEADS * HEAD_SIZE), jnp.float32) / math.sqrt(MODEL_WIDTH)
    return score_matrix.astype(jnp.bfloat16)


def draw_w_keyval(key, part):
    key = jax.random.fold_in(key, 4)
    score_matrix = jax.random.truncated_normal(key, -4.0, 4.0, (MODEL_WIDTH, 2 * KEYVAL_HEADS * HEAD_SIZE), jnp.float32) / math.sqrt(MODEL_WIDTH)
    return score_matrix.astype(jnp.bfloat16)


def draw_step_lengths(key, part):
    key = jax.random.fold_in(key, 5)
    key_draw, key_pick = jax.random.split(key)
    lengths = jax.random.randint(key_draw, (SAMPLES,), 1, STEP_SLOTS + 1, jnp.int32)
    full_index = jax.random.randint(key_pick, (), 0, SAMPLES, jnp.int32)
    return lengths.at[full_index].set(STEP_SLOTS)


def place_ends(values, own_key, smallest, top_value):
    place = [jax.random.randint(jax.random.fold_in(own_key, axis), (), 0, length) for axis, length in enumerate(values.shape)]
    main_axis = values.shape.index(max(values.shape))
    neighbour = place[:main_axis] + [(place[main_axis] + 1) % values.shape[main_axis]] + place[main_axis + 1:]
    return values.at[tuple(place)].set(smallest).at[tuple(neighbour)].set(top_value)


def setup_inputs(seed: int = 0) -> dict:
    key_list = jax.random.split(jax.random.key(seed), 8)
    ctx_hidden = draw_ctx_hidden(jax.random.fold_in(key_list[7], 71), 0)
    step_hidden = draw_step_hidden(jax.random.fold_in(key_list[7], 71), 0)
    norm_gain = jnp.clip(1.0 + 0.18 * jax.random.normal(key_list[2], (MODEL_WIDTH,), jnp.float32), 0.1, 1.9)
    w_query = draw_w_query(jax.random.fold_in(key_list[7], 71), 0)
    w_keyval = draw_w_keyval(jax.random.fold_in(key_list[7], 71), 0)
    step_lengths = draw_step_lengths(jax.random.fold_in(key_list[7], 71), 0)
    step_mask = place_ends((jax.random.randint(key_list[6], (SAMPLES, STEP_SLOTS, STEP_SLOTS), 0, 4) < 3).astype(jnp.int32), jax.random.fold_in(key_list[6], 1), 0, 1)
    return dict(ctx_hidden=ctx_hidden, step_hidden=step_hidden, norm_gain=norm_gain, w_query=w_query, w_keyval=w_keyval, step_lengths=step_lengths, step_mask=step_mask)


NEG_FILL = -1e+30

def rms_norm(hidden_rows, norm_gain):
    widened = hidden_rows.astype(jnp.float32)
    inverse = lax.rsqrt(lax.optimization_barrier(jnp.mean(widened * widened, axis=-1, keepdims=True)) + 1e-06)
    return (widened * inverse * norm_gain).astype(jnp.bfloat16)

def rounded(values):
    return lax.optimization_barrier(values.astype(jnp.bfloat16))

def reference(ctx_hidden, step_hidden, norm_gain, w_query, w_keyval, step_lengths, step_mask):
    head_groups = QUERY_HEADS // KEYVAL_HEADS
    score_scale = 1.0 / math.sqrt(HEAD_SIZE)
    normed_context = rms_norm(ctx_hidden, norm_gain)
    problem_keyval = rounded(jnp.dot(normed_context, w_keyval, preferred_element_type=jnp.float32))
    problem_keyval = problem_keyval.astype(jnp.float32).reshape(CONTEXT_TOKENS, 2, KEYVAL_HEADS, HEAD_SIZE)
    context_keys = problem_keyval[:, 0]
    context_values = problem_keyval[:, 1]
    positions = jnp.arange(STEP_SLOTS, dtype=jnp.int32)
    causal = positions[None, :] <= positions[:, None]
    diagonal = positions[None, :] == positions[:, None]
    block_extent = 4

    def one_block(inputs):
        hidden_block, length_block, mask_block = inputs
        normed_step = rms_norm(hidden_block.reshape(block_extent * STEP_SLOTS, MODEL_WIDTH), norm_gain)
        query_block = rounded(jnp.dot(normed_step, w_query, preferred_element_type=jnp.float32))
        query_block = query_block.astype(jnp.float32).reshape(block_extent, STEP_SLOTS, KEYVAL_HEADS, head_groups, HEAD_SIZE)
        solution_keyval = rounded(jnp.dot(normed_step, w_keyval, preferred_element_type=jnp.float32))
        solution_keyval = solution_keyval.astype(jnp.float32).reshape(block_extent, STEP_SLOTS, 2, KEYVAL_HEADS, HEAD_SIZE)
        step_keys = solution_keyval[:, :, 0]
        step_values = solution_keyval[:, :, 1]
        ctx_scores = jnp.einsum('bthgd,nhd->bthgn', query_block, context_keys) * score_scale
        step_scores = jnp.einsum('bthgd,buhd->bthgu', query_block, step_keys) * score_scale
        allowed = causal[None] & (diagonal[None] | (mask_block == 1)) & (positions[None, None, :] < length_block[:, None, None])
        step_scores = jnp.where(allowed[:, :, None, None, :], step_scores, NEG_FILL)
        row_top = jnp.maximum(ctx_scores.max(-1), step_scores.max(-1))
        ctx_weights = jnp.exp(ctx_scores - row_top[..., None])
        step_weights = jnp.exp(step_scores - row_top[..., None])
        weight_sum = ctx_weights.sum(-1) + step_weights.sum(-1)
        attended = jnp.einsum('bthgn,nhd->bthgd', rounded(ctx_weights).astype(jnp.float32), context_values)
        attended = attended + jnp.einsum('bthgu,buhd->bthgd', rounded(step_weights).astype(jnp.float32), step_values)
        attended = attended / weight_sum[..., None]
        live_rows = positions[None, :] < length_block[:, None]
        attended = jnp.where(live_rows[:, :, None, None, None], attended, 0.0)
        return attended.reshape(block_extent, STEP_SLOTS, QUERY_HEADS * HEAD_SIZE).astype(jnp.bfloat16)
    blocks = SAMPLES // block_extent
    result = lax.map(one_block, (step_hidden.reshape(blocks, block_extent, STEP_SLOTS, MODEL_WIDTH), step_lengths.reshape(blocks, block_extent), step_mask.reshape(blocks, block_extent, STEP_SLOTS, STEP_SLOTS)))
    return result.reshape(SAMPLES, STEP_SLOTS, QUERY_HEADS * HEAD_SIZE)
```

```python
import functools
import math

import jax
import jax.numpy as jnp
from jax import lax
from jax.experimental import pallas as pl
from jax.experimental.pallas import tpu as pltpu
from jax.sharding import PartitionSpec as P

HEAD_SIZE = 128
KEYVAL_HEADS = 2
NEG_FILL = -1e30
MESH = pl.DeviceIdType.MESH


def split_heads(head_groups):
    widths = []
    while head_groups > 0:
        widths.append(min(2, head_groups))
        head_groups -= widths[-1]
    return widths


def norm_rows(src, dst, gain_ref, count, first, block=64):
    def body(i, carry):
        rows = pl.ds(pl.multiple_of(first + i * block, block), block)
        widened = src[rows, :].astype(jnp.float32)
        inverse = lax.rsqrt(jnp.mean(widened * widened, axis=-1, keepdims=True) + 1e-06)
        dst[rows, :] = (widened * inverse * gain_ref[...]).astype(jnp.bfloat16)
        return carry

    lax.fori_loop(0, count // block, body, 0)


def kernel(
    n_dev, samples, slots, widths, ctx_ref, step_ref, gain_ref, wq_ref, wkv_ref, lens_ref, mask_ref,
    out_ref, rows_buf, ctx_buf, wkv_buf, *rest
):
    groups = len(widths)
    wq_bufs = rest[:groups]
    (ckv_buf, skv_buf, q_buf, aux_buf, part_buf,
     recv_sem, send_sem, local_sem, pair_recv, out_recv) = rest[groups:]
    own_rows = samples * slots
    shard = wkv_ref.shape[0]
    ctx_rows = ctx_ref.shape[0]
    half_cols = sum(widths) * HEAD_SIZE
    line = n_dev // 2

    g = lax.axis_index("grp")
    d = lax.axis_index("dev")
    core = lax.rem(g, 2)
    head = lax.rem(g // 2, 2)
    a = d // 2
    b = lax.rem(d, 2)
    sibling = (g + 1 - 2 * core, d)
    pair = (g + 2 - 4 * head, d)
    across = (g, 2 * a + 1 - b)

    def along(t):
        return 2 * lax.rem(a + t, line) + b

    barrier = pltpu.get_barrier_semaphore()
    friends = [sibling, pair, across] + [(g, along(t)) for t in range(1, line)]
    for friend in friends:
        pl.semaphore_signal(barrier, inc=1, device_id=friend, device_id_type=MESH)
    pl.semaphore_wait(barrier, len(friends))

    pending = []

    def send(src, dst, sem, target):
        copy = pltpu.make_async_remote_copy(
            src_ref=src, dst_ref=dst, send_sem=send_sem.at[len(pending)], recv_sem=sem,
            device_id=target, device_id_type=MESH,
        )
        copy.start()
        pending.append(copy)

    class Gather:
        def __init__(self, kind, buf, size):
            self.kind, self.buf, self.size = kind, buf, size
            self.halves = 2 if size % 32 == 0 else 1
            self.piece = size // self.halves
            self.mine = core if self.halves == 2 else 0

        def at(self, src, half):
            start = src * self.size + half * self.piece
            return self.buf.at[pl.ds(pl.multiple_of(start, 16), self.piece)]

        def sem(self, src, half):
            return recv_sem.at[self.kind, half, src]

        def wait(self, src, half):
            ref = self.at(src, half)
            pltpu.make_async_copy(ref, ref, self.sem(src, half)).wait()

        def forward(self, src, target):
            ref = self.at(src, self.mine)
            send(ref, ref, self.sem(src, self.mine), target)

        def start(self, sources):
            for target in [(g, along(t)) for t in range(1, line)] + [across]:
                send(sources, self.at(d, self.mine), self.sem(d, self.mine), target)

        def along_line(self):
            for t in range(1, line):
                src = along(t)
                self.wait(src, self.mine)
                self.forward(src, across)
                if self.halves == 2:
                    self.forward(src, sibling)

        def across_line(self):
            for t in range(line):
                src = 2 * lax.rem(a + t, line) + 1 - b
                self.wait(src, self.mine)
                if self.halves == 2:
                    self.forward(src, sibling)

        def finish(self):
            if self.halves == 2:
                for t in range(1, n_dev):
                    self.wait(lax.rem(d + t, n_dev), 1 - self.mine)

    send(step_ref, rows_buf.at[pl.ds(0, own_rows)], pair_recv.at[0], pair)

    gathers = [Gather(0, wkv_buf, shard)]
    gathers += [Gather(1 + i, wq_bufs[i], shard) for i in range(groups)]
    ctx_gather = Gather(1 + groups, ckv_buf, ctx_rows)

    locals_ = []

    def local(src, dst):
        copy = pltpu.make_async_copy(src, dst, local_sem.at[len(locals_)])
        copy.start()
        locals_.append(copy)

    own_shard = pl.ds(pl.multiple_of(d * shard, 16), shard)
    for part in range(2):
        cols = pl.ds(pl.multiple_of((part * KEYVAL_HEADS + head) * HEAD_SIZE, HEAD_SIZE), HEAD_SIZE)
        local(wkv_ref.at[:, cols], wkv_buf.at[own_shard, pl.ds(part * HEAD_SIZE, HEAD_SIZE)])
    local(step_ref, rows_buf.at[pl.ds(own_rows, own_rows)])
    col = 0
    starts = []
    for i in range(groups):
        width = widths[i] * HEAD_SIZE
        cols = pl.ds(pl.multiple_of(head * half_cols + col, HEAD_SIZE), width)
        local(wq_ref.at[:, cols], wq_bufs[i].at[own_shard])
        starts.append(cols)
        col += width
    locals_[0].wait()
    locals_[1].wait()
    gathers[0].start(gathers[0].at(d, gathers[0].mine))
    for i in range(groups):
        gather = gathers[1 + i]
        first = pl.multiple_of(gather.mine * gather.piece, 16)
        gather.start(wq_ref.at[pl.ds(first, gather.piece), starts[i]])

    t_at = lax.broadcasted_iota(jnp.int32, (slots, slots), 0)
    u_at = lax.broadcasted_iota(jnp.int32, (slots, slots), 1)
    for s in range(samples):
        length = lens_ref[s]
        allowed = (u_at <= t_at) & ((u_at == t_at) | (mask_ref[s] == 1)) & (u_at < length)
        rows = pl.ds(own_rows + s * slots, slots)
        aux_buf[rows, 0:slots] = jnp.where(allowed, 1.0, 0.0).astype(jnp.bfloat16)
        aux_buf[rows, slots:2 * slots] = jnp.where(t_at < length, 1.0, 0.0).astype(jnp.bfloat16)
    send(aux_buf.at[pl.ds(own_rows, own_rows)], aux_buf.at[pl.ds(0, own_rows)], pair_recv.at[1], pair)

    norm_rows(ctx_ref, ctx_buf, gain_ref, ctx_rows, 0)
    gathers[0].along_line()
    locals_[2].wait()
    norm_rows(rows_buf, rows_buf, gain_ref, own_rows, own_rows)
    gathers[0].across_line()
    gathers[1].along_line()
    gathers[0].finish()
    own_ckv = jnp.dot(ctx_buf[...], wkv_buf[...], preferred_element_type=jnp.float32)
    ckv_buf[pl.ds(pl.multiple_of(d * ctx_rows, 16), ctx_rows), :] = own_ckv.astype(jnp.bfloat16)
    ctx_gather.start(ctx_gather.at(d, ctx_gather.mine))
    gathers[1].across_line()
    ctx_gather.along_line()
    ctx_gather.across_line()

    for i in range(2):
        ref = (rows_buf, aux_buf)[i].at[pl.ds(0, own_rows)]
        pltpu.make_async_copy(ref, ref, pair_recv.at[i]).wait()
    norm_rows(rows_buf, rows_buf, gain_ref, own_rows, 0)
    skv_buf[...] = jnp.dot(
        rows_buf[...], wkv_buf[...], preferred_element_type=jnp.float32
    ).astype(jnp.bfloat16)
    ctx_gather.finish()

    score_scale = 1.0 / math.sqrt(HEAD_SIZE)
    contract_last = (((1,), (1,)), ((), ()))

    def attend(heads, sample):
        rows = pl.ds(pl.multiple_of(sample * slots, slots), slots)
        q = q_buf[0:heads, rows, :].reshape(heads * slots, HEAD_SIZE)
        ctx_scores = lax.dot_general(
            q, ckv_buf[:, 0:HEAD_SIZE], contract_last, preferred_element_type=jnp.float32
        ) * score_scale
        step_scores = lax.dot_general(
            q, skv_buf[rows, 0:HEAD_SIZE], contract_last, preferred_element_type=jnp.float32
        ) * score_scale
        allowed = aux_buf[rows, 0:slots].astype(jnp.float32) > 0.5
        step_scores = jnp.where(
            allowed[None], step_scores.reshape(heads, slots, slots), NEG_FILL
        ).reshape(heads * slots, slots)
        top = jnp.maximum(
            jnp.max(ctx_scores, axis=-1, keepdims=True), jnp.max(step_scores, axis=-1, keepdims=True)
        )
        ctx_weights = jnp.exp(ctx_scores - top)
        step_weights = jnp.exp(step_scores - top)
        weight_sum = jnp.sum(ctx_weights, axis=-1, keepdims=True)
        weight_sum += jnp.sum(step_weights, axis=-1, keepdims=True)
        attended = jnp.dot(
            ctx_weights.astype(jnp.bfloat16), ckv_buf[:, HEAD_SIZE:], preferred_element_type=jnp.float32
        )
        attended += jnp.dot(
            step_weights.astype(jnp.bfloat16), skv_buf[rows, HEAD_SIZE:], preferred_element_type=jnp.float32
        )
        attended = (attended / weight_sum).reshape(heads, slots, HEAD_SIZE)
        live = aux_buf[rows, slots:slots + 1].astype(jnp.float32) > 0.5
        return jnp.where(live[None], attended, 0.0).astype(jnp.bfloat16)

    col = 0
    for i in range(groups):
        heads = widths[i]
        if i + 1 < groups:
            gathers[2 + i].along_line()
        locals_[3 + i].wait()
        gathers[1 + i].finish()
        q = jnp.dot(rows_buf[...], wq_bufs[i][...], preferred_element_type=jnp.float32)
        for h in range(heads):
            q_buf[h] = q[:, h * HEAD_SIZE:(h + 1) * HEAD_SIZE].astype(jnp.bfloat16)

        def for_pair(sample, carry, heads=heads, col=col):
            attended = attend(heads, sample)
            rows = pl.ds(pl.multiple_of(sample * slots, slots), slots)
            for h in range(heads):
                part_buf[rows, col + h * HEAD_SIZE:col + (h + 1) * HEAD_SIZE] = attended[h]
            return carry

        def for_own(sample, carry, heads=heads, col=col):
            attended = attend(heads, samples + sample)
            rows = pl.ds(pl.multiple_of(sample * slots, slots), slots)
            for h in range(heads):
                first = pl.multiple_of(head * half_cols + col + h * HEAD_SIZE, HEAD_SIZE)
                out_ref[rows, pl.ds(first, HEAD_SIZE)] = attended[h]
            return carry

        lax.fori_loop(0, samples, for_pair, 0)
        width = heads * HEAD_SIZE
        there = out_ref.at[:, pl.ds(pl.multiple_of(head * half_cols + col, HEAD_SIZE), width)]
        send(part_buf.at[:, pl.ds(col, width)], there, out_recv.at[i], pair)
        lax.fori_loop(0, samples, for_own, 0)
        col += width
        if i + 1 < groups:
            gathers[2 + i].across_line()

    col = 0
    for i in range(groups):
        width = widths[i] * HEAD_SIZE
        here = out_ref.at[:, pl.ds(pl.multiple_of((1 - head) * half_cols + col, HEAD_SIZE), width)]
        pltpu.make_async_copy(here, here, out_recv.at[i]).wait()
        col += width
    for copy in pending:
        copy.wait_send()


def local(ctx_hidden, step_hidden, norm_gain, w_query, w_keyval, step_lengths, step_mask, n_dev):
    samples, slots, features = step_hidden.shape
    own_rows = samples * slots
    query_cols = w_query.shape[1]
    widths = split_heads(query_cols // HEAD_SIZE // KEYVAL_HEADS)
    groups = len(widths)
    ctx_rows = ctx_hidden.shape[0]
    bf16 = jnp.bfloat16
    sends = (groups + 2) * (2 * n_dev) + 2 + groups
    vmem = pl.BlockSpec(memory_space=pltpu.VMEM)
    smem = pl.BlockSpec(memory_space=pltpu.SMEM)
    anywhere = pl.BlockSpec(memory_space=pl.ANY)
    out = pl.pallas_call(
        functools.partial(kernel, n_dev, samples, slots, widths),
        out_shape=jax.ShapeDtypeStruct((own_rows, query_cols), bf16),
        in_specs=[vmem, anywhere, vmem, anywhere, anywhere, smem, vmem],
        out_specs=vmem,
        scratch_shapes=[
            pltpu.VMEM((2 * own_rows, features), bf16),
            pltpu.VMEM((ctx_rows, features), bf16),
            pltpu.VMEM((features, 2 * HEAD_SIZE), bf16),
        ]
        + [pltpu.VMEM((features, width * HEAD_SIZE), bf16) for width in widths]
        + [
            pltpu.VMEM((n_dev * ctx_rows, 2 * HEAD_SIZE), bf16),
            pltpu.VMEM((2 * own_rows, 2 * HEAD_SIZE), bf16),
            pltpu.VMEM((max(widths), 2 * own_rows, HEAD_SIZE), bf16),
            pltpu.VMEM((2 * own_rows, 2 * slots), bf16),
            pltpu.VMEM((own_rows, query_cols // 2), bf16),
            pltpu.SemaphoreType.DMA((groups + 2, 2, n_dev)),
            pltpu.SemaphoreType.DMA((sends,)),
            pltpu.SemaphoreType.DMA((3 + groups,)),
            pltpu.SemaphoreType.DMA((2,)),
            pltpu.SemaphoreType.DMA((groups,)),
        ],
        compiler_params=pltpu.CompilerParams(
            collective_id=0, has_side_effects=True, vmem_limit_bytes=48 * 1024 * 1024
        ),
        name="shared_context_attention",
    )(
        ctx_hidden, step_hidden.reshape(own_rows, features), norm_gain.reshape(1, features),
        w_query, w_keyval, step_lengths, step_mask,
    )
    return out.reshape(samples, slots, query_cols)


def solution(mesh):
    placed = (
        P("dev", None),
        P(("grp", "dev"), None, None),
        P(),
        P("dev", None),
        P("dev", None),
        P(("grp", "dev")),
        P(("grp", "dev"), None, None),
    )
    return jax.shard_map(
        functools.partial(local, n_dev=mesh.shape["dev"]),
        mesh=mesh, in_specs=placed, out_specs=P(("grp", "dev"), None, None), check_vma=False,
    )
```

```python
import functools
import math

import jax
import jax.numpy as jnp
from jax import lax
from jax.experimental import pallas as pl
from jax.experimental.pallas import tpu as pltpu
from jax.sharding import PartitionSpec as P

HEAD_SIZE = 128
SLAB = 16
KEYVAL_HEADS = 2
NEG_FILL = -1e30
MESH = pl.DeviceIdType.MESH


def split_heads(head_groups):
    widths = []
    while head_groups > 0:
        widths.append(min(2, head_groups))
        head_groups -= widths[-1]
    return widths


def norm_rows(src, dst, gain_ref, count, first, block=64):
    def body(i, carry):
        rows = pl.ds(pl.multiple_of(first + i * block, block), block)
        widened = src[rows, :].astype(jnp.float32)
        inverse = lax.rsqrt(jnp.mean(widened * widened, axis=-1, keepdims=True) + 1e-06)
        dst[rows, :] = (widened * inverse * gain_ref[...]).astype(jnp.bfloat16)
        return carry

    lax.fori_loop(0, count // block, body, 0)


def kernel(
    n_dev, samples, slots, widths, ctx_hbm, step_ref, gain_hbm, wq_ref, wkv_ref, lens_ref, mask_hbm,
    out_ref, ctx_ref, gain_tiles, gain_ref, mask_ref, rows_buf, ctx_buf, wkv_buf, *rest
):
    groups = len(widths)
    wq_bufs = rest[:groups]
    (ckv_buf, keyval_buf, q_buf, aux_buf, may_buf, part_buf,
     recv_sem, send_sem, local_sem, pair_recv, out_recv) = rest[groups:]
    own_rows = samples * slots
    shard = wkv_ref.shape[0]
    ctx_rows = ctx_ref.shape[0]
    half_cols = sum(widths) * HEAD_SIZE
    line = n_dev // 2

    g = lax.axis_index("grp")
    d = lax.axis_index("dev")
    core = lax.rem(g, 2)
    head = lax.rem(g // 2, 2)
    a = d // 2
    b = lax.rem(d, 2)
    sibling = (g + 1 - 2 * core, d)
    pair = (g + 2 - 4 * head, d)
    across = (g, 2 * a + 1 - b)

    def along(t):
        return 2 * lax.rem(a + t, line) + b

    barrier = pltpu.get_barrier_semaphore()
    friends = [sibling, pair, across] + [(g, along(t)) for t in range(1, line)]
    for friend in friends:
        pl.semaphore_signal(barrier, inc=1, device_id=friend, device_id_type=MESH)
    pl.semaphore_wait(barrier, len(friends))

    pending = []

    def send(src, dst, sem, target):
        copy = pltpu.make_async_remote_copy(
            src_ref=src, dst_ref=dst, send_sem=send_sem.at[len(pending)], recv_sem=sem,
            device_id=target, device_id_type=MESH,
        )
        copy.start()
        pending.append(copy)

    class Gather:
        def __init__(self, kind, buf, size):
            self.kind, self.buf, self.size = kind, buf, size
            self.halves = 2 if size % 32 == 0 else 1
            self.piece = size // self.halves
            self.mine = core if self.halves == 2 else 0

        def at(self, src, half):
            start = src * self.size + half * self.piece
            return self.buf.at[pl.ds(pl.multiple_of(start, 16), self.piece)]

        def sem(self, src, half):
            return recv_sem.at[self.kind, half, src]

        def wait(self, src, half):
            ref = self.at(src, half)
            pltpu.make_async_copy(ref, ref, self.sem(src, half)).wait()

        def forward(self, src, target):
            ref = self.at(src, self.mine)
            send(ref, ref, self.sem(src, self.mine), target)

        def starts(self, source):
            targets = [(g, along(t)) for t in range(1, line)]
            targets.insert(1, across)
            place, sem = self.at(d, self.mine), self.sem(d, self.mine)
            return [functools.partial(send, source, place, sem, target) for target in targets]

        def relay_along(self, t):
            src = along(t)
            self.wait(src, self.mine)
            self.forward(src, across)
            if self.halves == 2:
                self.forward(src, sibling)

        def relay_across(self, t):
            src = 2 * lax.rem(a + t, line) + 1 - b
            self.wait(src, self.mine)
            if self.halves == 2:
                self.forward(src, sibling)

        def along_line(self):
            return [functools.partial(self.relay_along, t) for t in range(1, line)]

        def across_line(self):
            return [functools.partial(self.relay_across, t) for t in range(line)]

        def finish(self):
            if self.halves == 2:
                for t in range(1, n_dev):
                    self.wait(lax.rem(d + t, n_dev), 1 - self.mine)

    slabs = own_rows // SLAB

    def send_slab(i):
        rows = pl.ds(i * SLAB, SLAB)
        send(step_ref.at[rows], rows_buf.at[rows], pair_recv.at[i], pair)

    def run(*lists):
        lists = [list(events) for events in lists]
        while any(lists):
            for events in lists:
                if events:
                    events.pop(0)()

    gathers = [Gather(0, wkv_buf, shard)]
    gathers += [Gather(1 + i, wq_bufs[i], shard) for i in range(groups)]
    ctx_gather = Gather(1 + groups, ckv_buf, ctx_rows)

    locals_ = []

    def local(src, dst):
        copy = pltpu.make_async_copy(src, dst, local_sem.at[len(locals_)])
        copy.start()
        locals_.append(copy)

    own_shard = pl.ds(pl.multiple_of(d * shard, 16), shard)
    for part in range(2):
        cols = pl.ds(pl.multiple_of((part * KEYVAL_HEADS + head) * HEAD_SIZE, HEAD_SIZE), HEAD_SIZE)
        local(wkv_ref.at[:, cols], wkv_buf.at[own_shard, pl.ds(part * HEAD_SIZE, HEAD_SIZE)])
    local(step_ref, rows_buf.at[pl.ds(own_rows, own_rows)])
    small = [(ctx_hbm, ctx_ref), (gain_hbm, gain_tiles), (mask_hbm, mask_ref)]
    for src, dst in small:
        local(src, dst)
    col = 0
    starts = []
    for i in range(groups):
        width = widths[i] * HEAD_SIZE
        cols = pl.ds(pl.multiple_of(head * half_cols + col, HEAD_SIZE), width)
        local(wq_ref.at[:, cols], wq_bufs[i].at[own_shard])
        starts.append(cols)
        col += width
    locals_[0].wait()
    locals_[1].wait()
    pushes = []
    for i in range(groups):
        gather = gathers[1 + i]
        first = pl.multiple_of(gather.mine * gather.piece, 16)
        pushes.append(gather.starts(wq_ref.at[pl.ds(first, gather.piece), starts[i]]))
    pair_sends = [functools.partial(send_slab, i) for i in range(slabs)]
    third = -(-slabs // 3)
    run(gathers[0].starts(gathers[0].at(d, gathers[0].mine)) + pushes[0], pair_sends[:third])

    t_at = lax.broadcasted_iota(jnp.int32, (slots, slots), 0)
    u_at = lax.broadcasted_iota(jnp.int32, (slots, slots), 1)
    for copy in locals_[3:6]:
        copy.wait()
    for i in range(gain_tiles.shape[0]):
        gain_ref[:, i * HEAD_SIZE:(i + 1) * HEAD_SIZE] = gain_tiles[i:i + 1, :]
    for s in range(samples):
        length = lens_ref[s]
        allowed = (u_at <= t_at) & ((u_at == t_at) | (mask_ref[s] == 1)) & (u_at < length)
        rows = pl.ds(own_rows + s * slots, slots)
        aux_buf[rows, 0:slots] = jnp.where(allowed, 1.0, 0.0).astype(jnp.bfloat16)
        aux_buf[rows, slots:2 * slots] = jnp.where(t_at < length, 1.0, 0.0).astype(jnp.bfloat16)
    send(aux_buf.at[pl.ds(own_rows, own_rows)], aux_buf.at[pl.ds(0, own_rows)], pair_recv.at[slabs], pair)

    def expand(group):
        for s in range(samples):
            at = slice(s * slots, (s + 1) * slots)
            rows = slice(group * own_rows + s * slots, group * own_rows + (s + 1) * slots)
            may_buf[rows, at] = aux_buf[rows, 0:slots].astype(jnp.float32)

    all_ctx = n_dev * ctx_rows

    def project_step(group):
        rows = pl.ds(group * own_rows, own_rows)
        keyval_buf[group, pl.ds(all_ctx, own_rows), :] = jnp.dot(
            rows_buf[rows, :], wkv_buf[...], preferred_element_type=jnp.float32
        ).astype(jnp.bfloat16)

    def project_query(i, first, count):
        rows = pl.ds(first, count)
        q = jnp.dot(rows_buf[rows, :], wq_bufs[i][...], preferred_element_type=jnp.float32)
        for h in range(widths[i]):
            q_buf[h, rows, :] = q[:, h * HEAD_SIZE:(h + 1) * HEAD_SIZE].astype(jnp.bfloat16)

    score_scale = 1.0 / math.sqrt(HEAD_SIZE)
    contract_last = (((1,), (1,)), ((), ()))
    firsts = [sum(widths[:i]) * HEAD_SIZE for i in range(groups)]

    def attend(i, group):
        heads = widths[i]
        rows = pl.ds(group * own_rows, own_rows)
        q = q_buf[0:heads, rows, :].reshape(heads * own_rows, HEAD_SIZE)
        scores = lax.dot_general(
            q, keyval_buf[group, :, 0:HEAD_SIZE], contract_last, preferred_element_type=jnp.float32
        ) * score_scale
        may = may_buf[rows, :] > 0.5
        step_scores = scores[:, all_ctx:].reshape(heads, own_rows, own_rows)
        step_scores = jnp.where(may[None], step_scores, NEG_FILL).reshape(heads * own_rows, own_rows)
        ctx_scores = scores[:, 0:all_ctx]
        top = jnp.maximum(
            jnp.max(ctx_scores, axis=-1, keepdims=True), jnp.max(step_scores, axis=-1, keepdims=True)
        )
        ctx_weights = jnp.exp(ctx_scores - top)
        step_weights = jnp.exp(step_scores - top)
        weight_sum = jnp.sum(ctx_weights, axis=-1, keepdims=True)
        weight_sum += jnp.sum(step_weights, axis=-1, keepdims=True)
        attended = jnp.dot(
            ctx_weights.astype(jnp.bfloat16), keyval_buf[group, pl.ds(0, all_ctx), HEAD_SIZE:],
            preferred_element_type=jnp.float32,
        )
        attended += jnp.dot(
            step_weights.astype(jnp.bfloat16), keyval_buf[group, pl.ds(all_ctx, own_rows), HEAD_SIZE:],
            preferred_element_type=jnp.float32,
        )
        attended = (attended / weight_sum).reshape(heads, own_rows, HEAD_SIZE)
        live = aux_buf[rows, slots:slots + 1].astype(jnp.float32) > 0.5
        attended = jnp.where(live[None], attended, 0.0).astype(jnp.bfloat16)
        for h in range(heads):
            col = firsts[i] + h * HEAD_SIZE
            if group == 0:
                part_buf[:, col:col + HEAD_SIZE] = attended[h]
            else:
                first = pl.multiple_of(head * half_cols + col, HEAD_SIZE)
                out_ref[:, pl.ds(first, HEAD_SIZE)] = attended[h]
        if group == 0:
            width = heads * HEAD_SIZE
            first = pl.multiple_of(head * half_cols + firsts[i], HEAD_SIZE)
            here = part_buf.at[:, pl.ds(firsts[i], width)]
            send(here, out_ref.at[:, pl.ds(first, width)], out_recv.at[i], pair)

    may_buf[...] = jnp.zeros_like(may_buf)
    expand(1)
    norm_rows(ctx_ref, ctx_buf, gain_ref, ctx_rows, 0)
    run(gathers[0].along_line(), pushes[1], pair_sends[third:2 * third])
    locals_[2].wait()
    norm_rows(rows_buf, rows_buf, gain_ref, own_rows, own_rows)
    run(gathers[0].across_line(), gathers[1].along_line(), pushes[2], pair_sends[2 * third:])
    gathers[0].finish()
    own_ckv = jnp.dot(ctx_buf[...], wkv_buf[...], preferred_element_type=jnp.float32)
    ckv_buf[pl.ds(pl.multiple_of(d * ctx_rows, 16), ctx_rows), :] = own_ckv.astype(jnp.bfloat16)
    run(ctx_gather.starts(ctx_gather.at(d, ctx_gather.mine)))
    project_step(1)
    run(gathers[1].across_line(), ctx_gather.along_line(), gathers[2].along_line(), sum(pushes[3:], []))
    run(ctx_gather.across_line())
    ctx_gather.finish()
    for group in range(2):
        keyval_buf[group, pl.ds(0, all_ctx), :] = ckv_buf[...]

    locals_[6].wait()
    gathers[1].finish()
    project_query(0, own_rows, own_rows)
    attend(0, 1)
    run(gathers[2].across_line(), gathers[3].along_line() if groups > 2 else [])
    for i in range(slabs):
        ref = rows_buf.at[pl.ds(i * SLAB, SLAB)]
        pltpu.make_async_copy(ref, ref, pair_recv.at[i]).wait()
    ref = aux_buf.at[pl.ds(0, own_rows)]
    pltpu.make_async_copy(ref, ref, pair_recv.at[slabs]).wait()
    norm_rows(rows_buf, rows_buf, gain_ref, own_rows, 0)
    expand(0)
    project_step(0)
    project_query(0, 0, own_rows)
    attend(0, 0)

    for i in range(1, groups):
        across_next = gathers[2 + i].across_line() if i + 1 < groups else []
        along_next = gathers[3 + i].along_line() if i + 2 < groups else []
        locals_[6 + i].wait()
        gathers[1 + i].finish()
        project_query(i, 0, 2 * own_rows)
        run(across_next[:2], along_next[:2])
        attend(i, 0)
        run(across_next[2:], along_next[2:])
        attend(i, 1)

    col = 0
    for i in range(groups):
        width = widths[i] * HEAD_SIZE
        here = out_ref.at[:, pl.ds(pl.multiple_of((1 - head) * half_cols + col, HEAD_SIZE), width)]
        pltpu.make_async_copy(here, here, out_recv.at[i]).wait()
        col += width
    for copy in pending:
        copy.wait_send()


def local(ctx_hidden, step_hidden, norm_gain, w_query, w_keyval, step_lengths, step_mask, n_dev):
    samples, slots, features = step_hidden.shape
    own_rows = samples * slots
    query_cols = w_query.shape[1]
    widths = split_heads(query_cols // HEAD_SIZE // KEYVAL_HEADS)
    groups = len(widths)
    ctx_rows = ctx_hidden.shape[0]
    bf16 = jnp.bfloat16
    sends = (groups + 2) * (2 * n_dev) + own_rows // SLAB + 1 + groups
    vmem = pl.BlockSpec(memory_space=pltpu.VMEM)
    smem = pl.BlockSpec(memory_space=pltpu.SMEM)
    anywhere = pl.BlockSpec(memory_space=pl.ANY)
    out = pl.pallas_call(
        functools.partial(kernel, n_dev, samples, slots, widths),
        out_shape=jax.ShapeDtypeStruct((own_rows, query_cols), bf16),
        in_specs=[anywhere] * 5 + [smem, anywhere],
        out_specs=vmem,
        scratch_shapes=[
            pltpu.VMEM((ctx_rows, features), bf16),
            pltpu.VMEM((features // HEAD_SIZE, HEAD_SIZE), jnp.float32),
            pltpu.VMEM((1, features), jnp.float32),
            pltpu.VMEM((samples, slots, slots), jnp.int32),
            pltpu.VMEM((2 * own_rows, features), bf16),
            pltpu.VMEM((ctx_rows, features), bf16),
            pltpu.VMEM((features, 2 * HEAD_SIZE), bf16),
        ]
        + [pltpu.VMEM((features, width * HEAD_SIZE), bf16) for width in widths]
        + [
            pltpu.VMEM((n_dev * ctx_rows, 2 * HEAD_SIZE), bf16),
            pltpu.VMEM((2, n_dev * ctx_rows + own_rows, 2 * HEAD_SIZE), bf16),
            pltpu.VMEM((max(widths), 2 * own_rows, HEAD_SIZE), bf16),
            pltpu.VMEM((2 * own_rows, 2 * slots), bf16),
            pltpu.VMEM((2 * own_rows, own_rows), jnp.float32),
            pltpu.VMEM((own_rows, query_cols // 2), bf16),
            pltpu.SemaphoreType.DMA((groups + 2, 2, n_dev)),
            pltpu.SemaphoreType.DMA((sends,)),
            pltpu.SemaphoreType.DMA((6 + groups,)),
            pltpu.SemaphoreType.DMA((own_rows // SLAB + 1,)),
            pltpu.SemaphoreType.DMA((groups,)),
        ],
        compiler_params=pltpu.CompilerParams(
            collective_id=0, has_side_effects=True, vmem_limit_bytes=62 * 1024 * 1024
        ),
        name="shared_context_attention",
    )(
        ctx_hidden, step_hidden.reshape(own_rows, features), norm_gain.reshape(features // HEAD_SIZE, HEAD_SIZE),
        w_query, w_keyval, step_lengths, step_mask,
    )
    return out.reshape(samples, slots, query_cols)


def solution(mesh):
    placed = (
        P("dev", None),
        P(("grp", "dev"), None, None),
        P(),
        P("dev", None),
        P("dev", None),
        P(("grp", "dev")),
        P(("grp", "dev"), None, None),
    )
    return jax.shard_map(
        functools.partial(local, n_dev=mesh.shape["dev"]),
        mesh=mesh, in_specs=placed, out_specs=P(("grp", "dev"), None, None), check_vma=False,
    )
```

```python
import functools
import math

import jax
import jax.numpy as jnp
from jax import lax
from jax.experimental import pallas as pl
from jax.experimental.pallas import tpu as pltpu
from jax.sharding import PartitionSpec as P

HEAD_SIZE = 128
SLAB = 16
KEYVAL_HEADS = 2
NEG_FILL = -1e30
MESH = pl.DeviceIdType.MESH


def split_heads(head_groups):
    widths = []
    while head_groups > 0:
        widths.append(min(2, head_groups))
        head_groups -= widths[-1]
    return widths


def norm_rows(src, dst, gain_ref, count, first, block=64):
    def body(i, carry):
        rows = pl.ds(pl.multiple_of(first + i * block, block), block)
        widened = src[rows, :].astype(jnp.float32)
        inverse = lax.rsqrt(jnp.mean(widened * widened, axis=-1, keepdims=True) + 1e-06)
        dst[rows, :] = (widened * inverse * gain_ref[...]).astype(jnp.bfloat16)
        return carry

    lax.fori_loop(0, count // block, body, 0)


def kernel(
    n_dev, samples, slots, widths, ctx_hbm, step_ref, gain_hbm, wq_ref, wkv_ref, lens_ref, mask_hbm,
    out_ref, ctx_ref, gain_tiles, gain_ref, mask_ref, rows_buf, ctx_buf, wkv_buf, *rest
):
    groups = len(widths)
    wq_bufs = rest[:groups]
    (ckv_buf, keyval_buf, q_buf, aux_buf, may_buf, part_buf,
     recv_sem, send_sem, local_sem, pair_recv, out_recv) = rest[groups:]
    own_rows = samples * slots
    shard = wkv_ref.shape[0]
    ctx_rows = ctx_ref.shape[0]
    half_cols = sum(widths) * HEAD_SIZE
    line = n_dev // 2

    g = lax.axis_index("grp")
    d = lax.axis_index("dev")
    core = lax.rem(g, 2)
    head = lax.rem(g // 2, 2)
    a = d // 2
    b = lax.rem(d, 2)
    sibling = (g + 1 - 2 * core, d)
    pair = (g + 2 - 4 * head, d)
    across = (g, 2 * a + 1 - b)

    def along(j):
        t = j + (a // (line // 2)) * (line - 2 * j)
        return 2 * lax.rem(a + t, line) + b

    relayed = line > 2
    at_end = (a == 0) | (a == line - 1)
    before_end = (a == 1) | (a == line - 2)
    end = (g, 2 * (a // (line // 2)) * (line - 1) + b)

    barrier = pltpu.get_barrier_semaphore()
    friends = [sibling, pair, across] + [(g, along(t)) for t in range(1, line)]
    for friend in friends:
        pl.semaphore_signal(barrier, inc=1, device_id=friend, device_id_type=MESH)
    pl.semaphore_wait(barrier, len(friends))

    pending = []

    def send(src, dst, sem, target, cond=None):
        copy = pltpu.make_async_remote_copy(
            src_ref=src, dst_ref=dst, send_sem=send_sem.at[len(pending)], recv_sem=sem,
            device_id=target, device_id_type=MESH,
        )
        if cond is None:
            copy.start()
        else:
            pl.when(cond)(copy.start)
        pending.append((copy, cond))

    class Gather:
        def __init__(self, kind, buf, size):
            self.kind, self.buf, self.size = kind, buf, size
            self.halves = 2 if size % 32 == 0 else 1
            self.piece = size // self.halves
            self.mine = core if self.halves == 2 else 0

        def at(self, src, half):
            start = src * self.size + half * self.piece
            return self.buf.at[pl.ds(pl.multiple_of(start, 16), self.piece)]

        def sem(self, src, half):
            return recv_sem.at[self.kind, half, src]

        def wait(self, src, half):
            ref = self.at(src, half)
            pltpu.make_async_copy(ref, ref, self.sem(src, half)).wait()

        def forward(self, src, target, cond=None):
            ref = self.at(src, self.mine)
            send(ref, ref, self.sem(src, self.mine), target, cond)

        def starts(self):
            events = []
            for j in range(1, line):
                cond = jnp.logical_not(at_end) if relayed and j == line - 1 else None
                events.append(functools.partial(self.forward, d, (g, along(j)), cond))
            events.insert(1, functools.partial(self.forward, d, across))
            return events

        def relay_along(self, t):
            src = along(t)
            self.wait(src, self.mine)
            if relayed and t == line - 2:
                self.forward(src, end, before_end)
            self.forward(src, across)
            if self.halves == 2:
                self.forward(src, sibling)

        def relay_across(self, t):
            src = (d if t == 0 else along(t)) + 1 - 2 * b
            self.wait(src, self.mine)
            if self.halves == 2:
                self.forward(src, sibling)

        def along_line(self):
            return [functools.partial(self.relay_along, t) for t in range(1, line)]

        def across_line(self):
            return [functools.partial(self.relay_across, t) for t in range(line)]

        def finish(self):
            if self.halves == 2:
                for t in range(1, n_dev):
                    self.wait(lax.rem(d + t, n_dev), 1 - self.mine)

    slabs = own_rows // SLAB

    def send_slab(i):
        rows = pl.ds(i * SLAB, SLAB)
        send(step_ref.at[rows], rows_buf.at[rows], pair_recv.at[i], pair)

    def run(*lists):
        lists = [list(events) for events in lists]
        while any(lists):
            for events in lists:
                if events:
                    events.pop(0)()

    gathers = [Gather(0, wkv_buf, shard)]
    gathers += [Gather(1 + i, wq_bufs[i], shard) for i in range(groups)]
    ctx_gather = Gather(1 + groups, ckv_buf, ctx_rows)

    locals_ = []

    def local(src, dst):
        copy = pltpu.make_async_copy(src, dst, local_sem.at[len(locals_)])
        copy.start()
        locals_.append(copy)

    own_shard = pl.ds(pl.multiple_of(d * shard, 16), shard)
    for part in range(2):
        cols = pl.ds(pl.multiple_of((part * KEYVAL_HEADS + head) * HEAD_SIZE, HEAD_SIZE), HEAD_SIZE)
        local(wkv_ref.at[:, cols], wkv_buf.at[own_shard, pl.ds(part * HEAD_SIZE, HEAD_SIZE)])
    local(step_ref, rows_buf.at[pl.ds(own_rows, own_rows)])
    small = [(ctx_hbm, ctx_ref), (gain_hbm, gain_tiles), (mask_hbm, mask_ref)]
    for src, dst in small:
        local(src, dst)
    col = 0
    for i in range(groups):
        width = widths[i] * HEAD_SIZE
        cols = pl.ds(pl.multiple_of(head * half_cols + col, HEAD_SIZE), width)
        local(wq_ref.at[:, cols], wq_bufs[i].at[own_shard])
        col += width
    locals_[0].wait()
    locals_[1].wait()
    pair_sends = [functools.partial(send_slab, i) for i in range(slabs)]
    run(gathers[0].starts(), pair_sends[:slabs // 3])
    locals_[6].wait()
    run(gathers[1].starts(), pair_sends[slabs // 3:])
    for copy in locals_[7:]:
        copy.wait()
    pushes = [gather.starts() for gather in gathers[1:]]

    t_at = lax.broadcasted_iota(jnp.int32, (slots, slots), 0)
    u_at = lax.broadcasted_iota(jnp.int32, (slots, slots), 1)
    for copy in locals_[3:6]:
        copy.wait()
    for i in range(gain_tiles.shape[0]):
        gain_ref[:, i * HEAD_SIZE:(i + 1) * HEAD_SIZE] = gain_tiles[i:i + 1, :]
    for s in range(samples):
        length = lens_ref[s]
        allowed = (u_at <= t_at) & ((u_at == t_at) | (mask_ref[s] == 1)) & (u_at < length)
        rows = pl.ds(own_rows + s * slots, slots)
        aux_buf[rows, 0:slots] = jnp.where(allowed, 1.0, 0.0).astype(jnp.bfloat16)
        aux_buf[rows, slots:2 * slots] = jnp.where(t_at < length, 1.0, 0.0).astype(jnp.bfloat16)
    send(aux_buf.at[pl.ds(own_rows, own_rows)], aux_buf.at[pl.ds(0, own_rows)], pair_recv.at[slabs], pair)

    def expand(group):
        for s in range(samples):
            at = slice(s * slots, (s + 1) * slots)
            rows = slice(group * own_rows + s * slots, group * own_rows + (s + 1) * slots)
            may_buf[rows, at] = aux_buf[rows, 0:slots].astype(jnp.float32)

    all_ctx = n_dev * ctx_rows

    def project_step(group):
        rows = pl.ds(group * own_rows, own_rows)
        keyval_buf[group, pl.ds(all_ctx, own_rows), :] = jnp.dot(
            rows_buf[rows, :], wkv_buf[...], preferred_element_type=jnp.float32
        ).astype(jnp.bfloat16)

    def project_query(i, first, count):
        rows = pl.ds(first, count)
        q = jnp.dot(rows_buf[rows, :], wq_bufs[i][...], preferred_element_type=jnp.float32)
        for h in range(widths[i]):
            q_buf[h, rows, :] = q[:, h * HEAD_SIZE:(h + 1) * HEAD_SIZE].astype(jnp.bfloat16)

    score_scale = 1.0 / math.sqrt(HEAD_SIZE)
    contract_last = (((1,), (1,)), ((), ()))
    firsts = [sum(widths[:i]) * HEAD_SIZE for i in range(groups)]

    def attend(i, group):
        heads = widths[i]
        rows = pl.ds(group * own_rows, own_rows)
        q = q_buf[0:heads, rows, :].reshape(heads * own_rows, HEAD_SIZE)
        scores = lax.dot_general(
            q, keyval_buf[group, :, 0:HEAD_SIZE], contract_last, preferred_element_type=jnp.float32
        ) * score_scale
        may = may_buf[rows, :] > 0.5
        step_scores = scores[:, all_ctx:].reshape(heads, own_rows, own_rows)
        step_scores = jnp.where(may[None], step_scores, NEG_FILL).reshape(heads * own_rows, own_rows)
        ctx_scores = scores[:, 0:all_ctx]
        top = jnp.maximum(
            jnp.max(ctx_scores, axis=-1, keepdims=True), jnp.max(step_scores, axis=-1, keepdims=True)
        )
        ctx_weights = jnp.exp(ctx_scores - top)
        step_weights = jnp.exp(step_scores - top)
        weight_sum = jnp.sum(ctx_weights, axis=-1, keepdims=True)
        weight_sum += jnp.sum(step_weights, axis=-1, keepdims=True)
        attended = jnp.dot(
            ctx_weights.astype(jnp.bfloat16), keyval_buf[group, pl.ds(0, all_ctx), HEAD_SIZE:],
            preferred_element_type=jnp.float32,
        )
        attended += jnp.dot(
            step_weights.astype(jnp.bfloat16), keyval_buf[group, pl.ds(all_ctx, own_rows), HEAD_SIZE:],
            preferred_element_type=jnp.float32,
        )
        attended = (attended / weight_sum).reshape(heads, own_rows, HEAD_SIZE)
        live = aux_buf[rows, slots:slots + 1].astype(jnp.float32) > 0.5
        attended = jnp.where(live[None], attended, 0.0).astype(jnp.bfloat16)
        for h in range(heads):
            col = firsts[i] + h * HEAD_SIZE
            if group == 0:
                part_buf[:, col:col + HEAD_SIZE] = attended[h]
            else:
                first = pl.multiple_of(head * half_cols + col, HEAD_SIZE)
                out_ref[:, pl.ds(first, HEAD_SIZE)] = attended[h]
        if group == 0:
            width = heads * HEAD_SIZE
            first = pl.multiple_of(head * half_cols + firsts[i], HEAD_SIZE)
            here = part_buf.at[:, pl.ds(firsts[i], width)]
            send(here, out_ref.at[:, pl.ds(first, width)], out_recv.at[i], pair)

    may_buf[...] = jnp.zeros_like(may_buf)
    expand(1)
    norm_rows(ctx_ref, ctx_buf, gain_ref, ctx_rows, 0)
    run(gathers[0].along_line(), pushes[1])
    locals_[2].wait()
    norm_rows(rows_buf, rows_buf, gain_ref, own_rows, own_rows)
    run(gathers[0].across_line(), gathers[1].along_line(), pushes[2])
    gathers[0].finish()
    own_ckv = jnp.dot(ctx_buf[...], wkv_buf[...], preferred_element_type=jnp.float32)
    ckv_buf[pl.ds(pl.multiple_of(d * ctx_rows, 16), ctx_rows), :] = own_ckv.astype(jnp.bfloat16)
    run(ctx_gather.starts())
    project_step(1)
    run(gathers[1].across_line(), ctx_gather.along_line(), gathers[2].along_line(), sum(pushes[3:], []))
    run(ctx_gather.across_line())
    ctx_gather.finish()
    for group in range(2):
        keyval_buf[group, pl.ds(0, all_ctx), :] = ckv_buf[...]

    gathers[1].finish()
    project_query(0, own_rows, own_rows)
    attend(0, 1)
    run(gathers[2].across_line(), gathers[3].along_line() if groups > 2 else [])
    for i in range(slabs):
        ref = rows_buf.at[pl.ds(i * SLAB, SLAB)]
        pltpu.make_async_copy(ref, ref, pair_recv.at[i]).wait()
    ref = aux_buf.at[pl.ds(0, own_rows)]
    pltpu.make_async_copy(ref, ref, pair_recv.at[slabs]).wait()
    norm_rows(rows_buf, rows_buf, gain_ref, own_rows, 0)
    expand(0)
    project_step(0)
    project_query(0, 0, own_rows)
    attend(0, 0)

    for i in range(1, groups):
        across_next = gathers[2 + i].across_line() if i + 1 < groups else []
        along_next = gathers[3 + i].along_line() if i + 2 < groups else []
        gathers[1 + i].finish()
        project_query(i, 0, 2 * own_rows)
        run(across_next[:2], along_next[:2])
        attend(i, 0)
        run(across_next[2:], along_next[2:])
        attend(i, 1)

    col = 0
    for i in range(groups):
        width = widths[i] * HEAD_SIZE
        here = out_ref.at[:, pl.ds(pl.multiple_of((1 - head) * half_cols + col, HEAD_SIZE), width)]
        pltpu.make_async_copy(here, here, out_recv.at[i]).wait()
        col += width
    for copy, cond in pending:
        if cond is None:
            copy.wait_send()
        else:
            pl.when(cond)(copy.wait_send)


def local(ctx_hidden, step_hidden, norm_gain, w_query, w_keyval, step_lengths, step_mask, n_dev):
    samples, slots, features = step_hidden.shape
    own_rows = samples * slots
    query_cols = w_query.shape[1]
    widths = split_heads(query_cols // HEAD_SIZE // KEYVAL_HEADS)
    groups = len(widths)
    ctx_rows = ctx_hidden.shape[0]
    bf16 = jnp.bfloat16
    sends = (groups + 2) * (2 * n_dev) + own_rows // SLAB + 1 + groups
    vmem = pl.BlockSpec(memory_space=pltpu.VMEM)
    smem = pl.BlockSpec(memory_space=pltpu.SMEM)
    anywhere = pl.BlockSpec(memory_space=pl.ANY)
    out = pl.pallas_call(
        functools.partial(kernel, n_dev, samples, slots, widths),
        out_shape=jax.ShapeDtypeStruct((own_rows, query_cols), bf16),
        in_specs=[anywhere] * 5 + [smem, anywhere],
        out_specs=vmem,
        scratch_shapes=[
            pltpu.VMEM((ctx_rows, features), bf16),
            pltpu.VMEM((features // HEAD_SIZE, HEAD_SIZE), jnp.float32),
            pltpu.VMEM((1, features), jnp.float32),
            pltpu.VMEM((samples, slots, slots), jnp.int32),
            pltpu.VMEM((2 * own_rows, features), bf16),
            pltpu.VMEM((ctx_rows, features), bf16),
            pltpu.VMEM((features, 2 * HEAD_SIZE), bf16),
        ]
        + [pltpu.VMEM((features, width * HEAD_SIZE), bf16) for width in widths]
        + [
            pltpu.VMEM((n_dev * ctx_rows, 2 * HEAD_SIZE), bf16),
            pltpu.VMEM((2, n_dev * ctx_rows + own_rows, 2 * HEAD_SIZE), bf16),
            pltpu.VMEM((max(widths), 2 * own_rows, HEAD_SIZE), bf16),
            pltpu.VMEM((2 * own_rows, 2 * slots), bf16),
            pltpu.VMEM((2 * own_rows, own_rows), jnp.float32),
            pltpu.VMEM((own_rows, query_cols // 2), bf16),
            pltpu.SemaphoreType.DMA((groups + 2, 2, n_dev)),
            pltpu.SemaphoreType.DMA((sends,)),
            pltpu.SemaphoreType.DMA((6 + groups,)),
            pltpu.SemaphoreType.DMA((own_rows // SLAB + 1,)),
            pltpu.SemaphoreType.DMA((groups,)),
        ],
        compiler_params=pltpu.CompilerParams(
            collective_id=0, has_side_effects=True, vmem_limit_bytes=62 * 1024 * 1024
        ),
        name="shared_context_attention",
    )(
        ctx_hidden, step_hidden.reshape(own_rows, features), norm_gain.reshape(features // HEAD_SIZE, HEAD_SIZE),
        w_query, w_keyval, step_lengths, step_mask,
    )
    return out.reshape(samples, slots, query_cols)


def solution(mesh):
    placed = (
        P("dev", None),
        P(("grp", "dev"), None, None),
        P(),
        P("dev", None),
        P("dev", None),
        P(("grp", "dev")),
        P(("grp", "dev"), None, None),
    )
    return jax.shard_map(
        functools.partial(local, n_dev=mesh.shape["dev"]),
        mesh=mesh, in_specs=placed, out_specs=P(("grp", "dev"), None, None), check_vma=False,
    )
```

```python
import functools
import math

import jax
import jax.numpy as jnp
from jax import lax
from jax.experimental import pallas as pl
from jax.experimental.pallas import tpu as pltpu
from jax.sharding import PartitionSpec as P

HEAD_SIZE = 128
SLAB = 16
KEYVAL_HEADS = 2
NEG_FILL = -1e30
MESH = pl.DeviceIdType.MESH


def split_heads(head_groups):
    widths = []
    while head_groups > 0:
        widths.append(min(2, head_groups))
        head_groups -= widths[-1]
    return widths


def norm_rows(src, dst, gain_ref, count, first, block=64):
    def body(i, carry):
        rows = pl.ds(pl.multiple_of(first + i * block, block), block)
        widened = src[rows, :].astype(jnp.float32)
        inverse = lax.rsqrt(jnp.mean(widened * widened, axis=-1, keepdims=True) + 1e-06)
        dst[rows, :] = (widened * inverse * gain_ref[...]).astype(jnp.bfloat16)
        return carry

    lax.fori_loop(0, count // block, body, 0)


def kernel(
    n_dev, samples, slots, widths, ctx_hbm, step_ref, gain_hbm, wq_ref, wkv_ref, lens_ref, mask_hbm,
    out_ref, ctx_ref, gain_tiles, gain_ref, mask_ref, rows_buf, ctx_buf, wkv_buf, *rest
):
    groups = len(widths)
    wq_bufs = rest[:groups]
    (ckv_buf, keyval_buf, q_buf, aux_buf, may_buf, part_buf,
     recv_sem, send_sem, local_sem, pair_recv, out_recv) = rest[groups:]
    own_rows = samples * slots
    shard = wkv_ref.shape[0]
    ctx_rows = ctx_ref.shape[0]
    half_cols = sum(widths) * HEAD_SIZE
    line = n_dev // 2

    g = lax.axis_index("grp")
    d = lax.axis_index("dev")
    core = lax.rem(g, 2)
    head = lax.rem(g // 2, 2)
    a = d // 2
    b = lax.rem(d, 2)
    sibling = (g + 1 - 2 * core, d)
    pair = (g + 2 - 4 * head, d)
    across = (g, 2 * a + 1 - b)

    def along(j):
        t = j + (a // (line // 2)) * (line - 2 * j)
        return 2 * lax.rem(a + t, line) + b

    relayed = line > 2
    at_end = (a == 0) | (a == line - 1)
    before_end = (a == 1) | (a == line - 2)
    end = (g, 2 * (a // (line // 2)) * (line - 1) + b)

    barrier = pltpu.get_barrier_semaphore()
    friends = [sibling, pair, across] + [(g, along(t)) for t in range(1, line)]
    for friend in friends:
        pl.semaphore_signal(barrier, inc=1, device_id=friend, device_id_type=MESH)
    pl.semaphore_wait(barrier, len(friends))

    pending = []

    def send(src, dst, sem, target, cond=None):
        copy = pltpu.make_async_remote_copy(
            src_ref=src, dst_ref=dst, send_sem=send_sem.at[len(pending)], recv_sem=sem,
            device_id=target, device_id_type=MESH,
        )
        if cond is None:
            copy.start()
        else:
            pl.when(cond)(copy.start)
        pending.append((copy, cond))

    class Gather:
        def __init__(self, kind, buf, size):
            self.kind, self.buf, self.size = kind, buf, size
            self.halves = 2 if size % 32 == 0 else 1
            self.piece = size // self.halves
            self.mine = core if self.halves == 2 else 0

        def at(self, src, half):
            start = src * self.size + half * self.piece
            return self.buf.at[pl.ds(pl.multiple_of(start, 16), self.piece)]

        def sem(self, src, half):
            return recv_sem.at[self.kind, half, src]

        def wait(self, src, half):
            ref = self.at(src, half)
            pltpu.make_async_copy(ref, ref, self.sem(src, half)).wait()

        def forward(self, src, target, cond=None):
            ref = self.at(src, self.mine)
            send(ref, ref, self.sem(src, self.mine), target, cond)

        def starts(self):
            events = self.to_line(d)
            events.insert(1, functools.partial(self.forward, d, across))
            return events

        def to_line(self, src):
            events = []
            for j in range(1, line):
                cond = jnp.logical_not(at_end) if relayed and j == line - 1 else None
                events.append(functools.partial(self.forward, src, (g, along(j)), cond))
            return events

        def spread_across(self):
            src = d + 1 - 2 * b
            self.wait(src, self.mine)
            if self.halves == 2:
                self.forward(src, sibling)
            for event in self.to_line(src):
                event()

        def take_along(self, t, other):
            src = along(t) + (1 - 2 * b if other else 0)
            self.wait(src, self.mine)
            if relayed and t == line - 2:
                self.forward(src, end, before_end)
            if self.halves == 2:
                self.forward(src, sibling)

        def take_line(self, other):
            return [functools.partial(self.take_along, t, other) for t in range(1, line)]

        def relay_along(self, t):
            src = along(t)
            self.wait(src, self.mine)
            if relayed and t == line - 2:
                self.forward(src, end, before_end)
            self.forward(src, across)
            if self.halves == 2:
                self.forward(src, sibling)

        def relay_across(self, t):
            src = (d if t == 0 else along(t)) + 1 - 2 * b
            self.wait(src, self.mine)
            if self.halves == 2:
                self.forward(src, sibling)

        def along_line(self):
            return [functools.partial(self.relay_along, t) for t in range(1, line)]

        def across_line(self):
            return [functools.partial(self.relay_across, t) for t in range(line)]

        def finish(self):
            if self.halves == 2:
                for t in range(1, n_dev):
                    self.wait(lax.rem(d + t, n_dev), 1 - self.mine)

    slabs = own_rows // SLAB

    def send_slab(i):
        rows = pl.ds(i * SLAB, SLAB)
        send(step_ref.at[rows], rows_buf.at[rows], pair_recv.at[i], pair)

    def run(*lists):
        lists = [list(events) for events in lists]
        while any(lists):
            for events in lists:
                if events:
                    events.pop(0)()

    gathers = [Gather(0, wkv_buf, shard)]
    gathers += [Gather(1 + i, wq_bufs[i], shard) for i in range(groups)]
    ctx_gather = Gather(1 + groups, ckv_buf, ctx_rows)

    locals_ = []

    def local(src, dst):
        copy = pltpu.make_async_copy(src, dst, local_sem.at[len(locals_)])
        copy.start()
        locals_.append(copy)

    own_shard = pl.ds(pl.multiple_of(d * shard, 16), shard)
    for part in range(2):
        cols = pl.ds(pl.multiple_of((part * KEYVAL_HEADS + head) * HEAD_SIZE, HEAD_SIZE), HEAD_SIZE)
        local(wkv_ref.at[:, cols], wkv_buf.at[own_shard, pl.ds(part * HEAD_SIZE, HEAD_SIZE)])
    local(step_ref, rows_buf.at[pl.ds(own_rows, own_rows)])
    small = [(ctx_hbm, ctx_ref), (gain_hbm, gain_tiles), (mask_hbm, mask_ref)]
    for src, dst in small:
        local(src, dst)
    col = 0
    for i in range(groups):
        width = widths[i] * HEAD_SIZE
        cols = pl.ds(pl.multiple_of(head * half_cols + col, HEAD_SIZE), width)
        local(wq_ref.at[:, cols], wq_bufs[i].at[own_shard])
        col += width
    locals_[0].wait()
    locals_[1].wait()
    last = gathers[-1]
    pair_sends = [functools.partial(send_slab, i) for i in range(slabs)]
    run(gathers[0].starts(), pair_sends[:slabs // 3])
    locals_[6].wait()
    run(gathers[1].starts(), pair_sends[slabs // 3:])
    for copy in locals_[7:]:
        copy.wait()
    pushes = [gather.starts() for gather in gathers[1:]]

    t_at = lax.broadcasted_iota(jnp.int32, (slots, slots), 0)
    u_at = lax.broadcasted_iota(jnp.int32, (slots, slots), 1)
    for copy in locals_[3:6]:
        copy.wait()
    for i in range(gain_tiles.shape[0]):
        gain_ref[:, i * HEAD_SIZE:(i + 1) * HEAD_SIZE] = gain_tiles[i:i + 1, :]
    for s in range(samples):
        length = lens_ref[s]
        allowed = (u_at <= t_at) & ((u_at == t_at) | (mask_ref[s] == 1)) & (u_at < length)
        rows = pl.ds(own_rows + s * slots, slots)
        aux_buf[rows, 0:slots] = jnp.where(allowed, 1.0, 0.0).astype(jnp.bfloat16)
        aux_buf[rows, slots:2 * slots] = jnp.where(t_at < length, 1.0, 0.0).astype(jnp.bfloat16)
    send(aux_buf.at[pl.ds(own_rows, own_rows)], aux_buf.at[pl.ds(0, own_rows)], pair_recv.at[slabs], pair)

    def expand(group):
        for s in range(samples):
            at = slice(s * slots, (s + 1) * slots)
            rows = slice(group * own_rows + s * slots, group * own_rows + (s + 1) * slots)
            may_buf[rows, at] = aux_buf[rows, 0:slots].astype(jnp.float32)

    all_ctx = n_dev * ctx_rows

    def project_step(group):
        rows = pl.ds(group * own_rows, own_rows)
        keyval_buf[group, pl.ds(all_ctx, own_rows), :] = jnp.dot(
            rows_buf[rows, :], wkv_buf[...], preferred_element_type=jnp.float32
        ).astype(jnp.bfloat16)

    def project_query(i, first, count):
        rows = pl.ds(first, count)
        q = jnp.dot(rows_buf[rows, :], wq_bufs[i][...], preferred_element_type=jnp.float32)
        for h in range(widths[i]):
            q_buf[h, rows, :] = q[:, h * HEAD_SIZE:(h + 1) * HEAD_SIZE].astype(jnp.bfloat16)

    score_scale = 1.0 / math.sqrt(HEAD_SIZE)
    contract_last = (((1,), (1,)), ((), ()))
    firsts = [sum(widths[:i]) * HEAD_SIZE for i in range(groups)]

    def attend(i, group):
        heads = widths[i]
        rows = pl.ds(group * own_rows, own_rows)
        q = q_buf[0:heads, rows, :].reshape(heads * own_rows, HEAD_SIZE)
        scores = lax.dot_general(
            q, keyval_buf[group, :, 0:HEAD_SIZE], contract_last, preferred_element_type=jnp.float32
        ) * score_scale
        may = may_buf[rows, :] > 0.5
        step_scores = scores[:, all_ctx:].reshape(heads, own_rows, own_rows)
        step_scores = jnp.where(may[None], step_scores, NEG_FILL).reshape(heads * own_rows, own_rows)
        ctx_scores = scores[:, 0:all_ctx]
        top = jnp.maximum(
            jnp.max(ctx_scores, axis=-1, keepdims=True), jnp.max(step_scores, axis=-1, keepdims=True)
        )
        ctx_weights = jnp.exp(ctx_scores - top)
        step_weights = jnp.exp(step_scores - top)
        weight_sum = jnp.sum(ctx_weights, axis=-1, keepdims=True)
        weight_sum += jnp.sum(step_weights, axis=-1, keepdims=True)
        attended = jnp.dot(
            ctx_weights.astype(jnp.bfloat16), keyval_buf[group, pl.ds(0, all_ctx), HEAD_SIZE:],
            preferred_element_type=jnp.float32,
        )
        attended += jnp.dot(
            step_weights.astype(jnp.bfloat16), keyval_buf[group, pl.ds(all_ctx, own_rows), HEAD_SIZE:],
            preferred_element_type=jnp.float32,
        )
        attended = (attended / weight_sum).reshape(heads, own_rows, HEAD_SIZE)
        live = aux_buf[rows, slots:slots + 1].astype(jnp.float32) > 0.5
        attended = jnp.where(live[None], attended, 0.0).astype(jnp.bfloat16)
        for h in range(heads):
            col = firsts[i] + h * HEAD_SIZE
            if group == 0:
                part_buf[:, col:col + HEAD_SIZE] = attended[h]
            else:
                first = pl.multiple_of(head * half_cols + col, HEAD_SIZE)
                out_ref[:, pl.ds(first, HEAD_SIZE)] = attended[h]
        if group == 0:
            width = heads * HEAD_SIZE
            first = pl.multiple_of(head * half_cols + firsts[i], HEAD_SIZE)
            here = part_buf.at[:, pl.ds(firsts[i], width)]
            send(here, out_ref.at[:, pl.ds(first, width)], out_recv.at[i], pair)

    may_buf[...] = jnp.zeros_like(may_buf)
    expand(1)
    norm_rows(ctx_ref, ctx_buf, gain_ref, ctx_rows, 0)
    run(gathers[0].along_line(), pushes[1])
    locals_[2].wait()
    norm_rows(rows_buf, rows_buf, gain_ref, own_rows, own_rows)
    run(gathers[0].across_line(), gathers[1].along_line(), pushes[2])
    gathers[0].finish()
    own_ckv = jnp.dot(ctx_buf[...], wkv_buf[...], preferred_element_type=jnp.float32)
    ckv_buf[pl.ds(pl.multiple_of(d * ctx_rows, 16), ctx_rows), :] = own_ckv.astype(jnp.bfloat16)
    run(ctx_gather.starts())
    project_step(1)
    run(gathers[1].across_line(), ctx_gather.along_line(), gathers[2].along_line(), sum(pushes[3:], []))
    last.spread_across()
    run(ctx_gather.across_line())
    ctx_gather.finish()
    for group in range(2):
        keyval_buf[group, pl.ds(0, all_ctx), :] = ckv_buf[...]

    gathers[1].finish()
    project_query(0, own_rows, own_rows)
    attend(0, 1)
    run(gathers[2].across_line(), gathers[3].along_line() if groups > 2 else [])
    for i in range(slabs):
        ref = rows_buf.at[pl.ds(i * SLAB, SLAB)]
        pltpu.make_async_copy(ref, ref, pair_recv.at[i]).wait()
    ref = aux_buf.at[pl.ds(0, own_rows)]
    pltpu.make_async_copy(ref, ref, pair_recv.at[slabs]).wait()
    norm_rows(rows_buf, rows_buf, gain_ref, own_rows, 0)
    expand(0)
    project_step(0)
    project_query(0, 0, own_rows)
    attend(0, 0)

    for i in range(1, groups):
        across_next = gathers[2 + i].across_line() if i + 2 < groups else []
        along_next = gathers[3 + i].along_line() if i + 3 < groups else []
        if i + 2 == groups:
            across_next = last.take_line(True)
        if i + 3 == groups:
            along_next = last.take_line(False)
        gathers[1 + i].finish()
        project_query(i, 0, 2 * own_rows)
        run(across_next[:2], along_next[:2])
        attend(i, 0)
        run(across_next[2:], along_next[2:])
        attend(i, 1)

    col = 0
    for i in range(groups):
        width = widths[i] * HEAD_SIZE
        here = out_ref.at[:, pl.ds(pl.multiple_of((1 - head) * half_cols + col, HEAD_SIZE), width)]
        pltpu.make_async_copy(here, here, out_recv.at[i]).wait()
        col += width
    for copy, cond in pending:
        if cond is None:
            copy.wait_send()
        else:
            pl.when(cond)(copy.wait_send)


def local(ctx_hidden, step_hidden, norm_gain, w_query, w_keyval, step_lengths, step_mask, n_dev):
    samples, slots, features = step_hidden.shape
    own_rows = samples * slots
    query_cols = w_query.shape[1]
    widths = split_heads(query_cols // HEAD_SIZE // KEYVAL_HEADS)
    groups = len(widths)
    ctx_rows = ctx_hidden.shape[0]
    bf16 = jnp.bfloat16
    sends = (groups + 2) * (2 * n_dev) + own_rows // SLAB + 1 + groups
    vmem = pl.BlockSpec(memory_space=pltpu.VMEM)
    smem = pl.BlockSpec(memory_space=pltpu.SMEM)
    anywhere = pl.BlockSpec(memory_space=pl.ANY)
    out = pl.pallas_call(
        functools.partial(kernel, n_dev, samples, slots, widths),
        out_shape=jax.ShapeDtypeStruct((own_rows, query_cols), bf16),
        in_specs=[anywhere] * 5 + [smem, anywhere],
        out_specs=vmem,
        scratch_shapes=[
            pltpu.VMEM((ctx_rows, features), bf16),
            pltpu.VMEM((features // HEAD_SIZE, HEAD_SIZE), jnp.float32),
            pltpu.VMEM((1, features), jnp.float32),
            pltpu.VMEM((samples, slots, slots), jnp.int32),
            pltpu.VMEM((2 * own_rows, features), bf16),
            pltpu.VMEM((ctx_rows, features), bf16),
            pltpu.VMEM((features, 2 * HEAD_SIZE), bf16),
        ]
        + [pltpu.VMEM((features, width * HEAD_SIZE), bf16) for width in widths]
        + [
            pltpu.VMEM((n_dev * ctx_rows, 2 * HEAD_SIZE), bf16),
            pltpu.VMEM((2, n_dev * ctx_rows + own_rows, 2 * HEAD_SIZE), bf16),
            pltpu.VMEM((max(widths), 2 * own_rows, HEAD_SIZE), bf16),
            pltpu.VMEM((2 * own_rows, 2 * slots), bf16),
            pltpu.VMEM((2 * own_rows, own_rows), jnp.float32),
            pltpu.VMEM((own_rows, query_cols // 2), bf16),
            pltpu.SemaphoreType.DMA((groups + 2, 2, n_dev)),
            pltpu.SemaphoreType.DMA((sends,)),
            pltpu.SemaphoreType.DMA((6 + groups,)),
            pltpu.SemaphoreType.DMA((own_rows // SLAB + 1,)),
            pltpu.SemaphoreType.DMA((groups,)),
        ],
        compiler_params=pltpu.CompilerParams(
            collective_id=0, has_side_effects=True, vmem_limit_bytes=62 * 1024 * 1024
        ),
        name="shared_context_attention",
    )(
        ctx_hidden, step_hidden.reshape(own_rows, features), norm_gain.reshape(features // HEAD_SIZE, HEAD_SIZE),
        w_query, w_keyval, step_lengths, step_mask,
    )
    return out.reshape(samples, slots, query_cols)


def solution(mesh):
    placed = (
        P("dev", None),
        P(("grp", "dev"), None, None),
        P(),
        P("dev", None),
        P("dev", None),
        P(("grp", "dev")),
        P(("grp", "dev"), None, None),
    )
    return jax.shard_map(
        functools.partial(local, n_dev=mesh.shape["dev"]),
        mesh=mesh, in_specs=placed, out_specs=P(("grp", "dev"), None, None), check_vma=False,
    )
```

```python
import functools
import math

import jax
import jax.numpy as jnp
from jax import lax
from jax.experimental import pallas as pl
from jax.experimental.pallas import tpu as pltpu
from jax.sharding import PartitionSpec as P

HEAD_SIZE = 128
SLAB = 16
KEYVAL_HEADS = 2
NEG_FILL = -1e30
MESH = pl.DeviceIdType.MESH


def split_heads(head_groups):
    widths = []
    while head_groups > 0:
        widths.append(min(2, head_groups))
        head_groups -= widths[-1]
    return widths


def norm_rows(src, dst, gain_ref, count, first, block=64):
    def body(i, carry):
        rows = pl.ds(pl.multiple_of(first + i * block, block), block)
        widened = src[rows, :].astype(jnp.float32)
        inverse = lax.rsqrt(jnp.mean(widened * widened, axis=-1, keepdims=True) + 1e-06)
        dst[rows, :] = (widened * inverse * gain_ref[...]).astype(jnp.bfloat16)
        return carry

    lax.fori_loop(0, count // block, body, 0)


def kernel(
    n_dev, samples, slots, widths, ctx_hbm, step_ref, gain_hbm, wq_ref, wkv_ref, lens_ref, mask_hbm,
    out_ref, ctx_ref, gain_tiles, gain_ref, mask_ref, rows_buf, ctx_buf, wkv_buf, *rest
):
    groups = len(widths)
    wq_bufs = rest[:groups]
    (ckv_buf, keyval_buf, q_buf, aux_buf, may_buf, part_buf,
     recv_sem, send_sem, local_sem, pair_recv, out_recv) = rest[groups:]
    own_rows = samples * slots
    shard = wkv_ref.shape[0]
    ctx_rows = ctx_ref.shape[0]
    half_cols = sum(widths) * HEAD_SIZE
    line = n_dev // 2

    g = lax.axis_index("grp")
    d = lax.axis_index("dev")
    core = lax.rem(g, 2)
    head = lax.rem(g // 2, 2)
    a = d // 2
    b = lax.rem(d, 2)
    sibling = (g + 1 - 2 * core, d)
    pair = (g + 2 - 4 * head, d)
    across = (g, 2 * a + 1 - b)

    def along(j):
        t = j + (a // (line // 2)) * (line - 2 * j)
        return 2 * lax.rem(a + t, line) + b

    relayed = line > 2
    at_end = (a == 0) | (a == line - 1)
    before_end = (a == 1) | (a == line - 2)
    end = (g, 2 * (a // (line // 2)) * (line - 1) + b)

    barrier = pltpu.get_barrier_semaphore()
    friends = [sibling, pair, across] + [(g, along(t)) for t in range(1, line)]
    for friend in friends:
        pl.semaphore_signal(barrier, inc=1, device_id=friend, device_id_type=MESH)
    pl.semaphore_wait(barrier, len(friends))

    pending = []

    def send(src, dst, sem, target, cond=None):
        copy = pltpu.make_async_remote_copy(
            src_ref=src, dst_ref=dst, send_sem=send_sem.at[len(pending)], recv_sem=sem,
            device_id=target, device_id_type=MESH,
        )
        if cond is None:
            copy.start()
        else:
            pl.when(cond)(copy.start)
        pending.append((copy, cond))

    class Gather:
        def __init__(self, kind, buf, size):
            self.kind, self.buf, self.size = kind, buf, size
            self.halves = 2 if size % 32 == 0 else 1
            self.piece = size // self.halves
            self.mine = core if self.halves == 2 else 0

        def at(self, src, half):
            start = src * self.size + half * self.piece
            return self.buf.at[pl.ds(pl.multiple_of(start, 16), self.piece)]

        def sem(self, src, half):
            return recv_sem.at[self.kind, half, src]

        def wait(self, src, half):
            ref = self.at(src, half)
            pltpu.make_async_copy(ref, ref, self.sem(src, half)).wait()

        def forward(self, src, target, cond=None):
            ref = self.at(src, self.mine)
            send(ref, ref, self.sem(src, self.mine), target, cond)

        def starts(self):
            events = []
            for j in range(1, line):
                cond = jnp.logical_not(at_end) if relayed and j == line - 1 else None
                events.append(functools.partial(self.forward, d, (g, along(j)), cond))
            events.insert(1, functools.partial(self.forward, d, across))
            return events

        def relay_along(self, t):
            src = along(t)
            self.wait(src, self.mine)
            if relayed and t == line - 2:
                self.forward(src, end, before_end)
            self.forward(src, across)
            if self.halves == 2:
                self.forward(src, sibling)

        def relay_across(self, t):
            src = (d if t == 0 else along(t)) + 1 - 2 * b
            self.wait(src, self.mine)
            if self.halves == 2:
                self.forward(src, sibling)

        def along_line(self):
            return [functools.partial(self.relay_along, t) for t in range(1, line)]

        def across_line(self):
            return [functools.partial(self.relay_across, t) for t in range(line)]

        def finish(self):
            if self.halves == 2:
                for t in range(1, n_dev):
                    self.wait(lax.rem(d + t, n_dev), 1 - self.mine)

    slabs = own_rows // SLAB

    def send_slab(i):
        rows = pl.ds(i * SLAB, SLAB)
        send(step_ref.at[rows], rows_buf.at[rows], pair_recv.at[i], pair)

    def run(*lists):
        lists = [list(events) for events in lists]
        while any(lists):
            for events in lists:
                if events:
                    events.pop(0)()

    gathers = [Gather(0, wkv_buf, shard)]
    gathers += [Gather(1 + i, wq_bufs[i], shard) for i in range(groups)]
    ctx_gather = Gather(1 + groups, ckv_buf, ctx_rows)

    locals_ = []

    def local(src, dst):
        copy = pltpu.make_async_copy(src, dst, local_sem.at[len(locals_)])
        copy.start()
        locals_.append(copy)

    own_shard = pl.ds(pl.multiple_of(d * shard, 16), shard)
    for part in range(2):
        cols = pl.ds(pl.multiple_of((part * KEYVAL_HEADS + head) * HEAD_SIZE, HEAD_SIZE), HEAD_SIZE)
        local(wkv_ref.at[:, cols], wkv_buf.at[own_shard, pl.ds(part * HEAD_SIZE, HEAD_SIZE)])
    local(step_ref, rows_buf.at[pl.ds(own_rows, own_rows)])
    small = [(ctx_hbm, ctx_ref), (gain_hbm, gain_tiles), (mask_hbm, mask_ref)]
    for src, dst in small:
        local(src, dst)
    col = 0
    for i in range(groups):
        width = widths[i] * HEAD_SIZE
        cols = pl.ds(pl.multiple_of(head * half_cols + col, HEAD_SIZE), width)
        local(wq_ref.at[:, cols], wq_bufs[i].at[own_shard])
        col += width
    locals_[0].wait()
    locals_[1].wait()
    pair_sends = [functools.partial(send_slab, i) for i in range(slabs)]
    run(gathers[0].starts(), pair_sends[:slabs // 3])
    locals_[6].wait()
    run(gathers[1].starts(), pair_sends[slabs // 3:])
    for copy in locals_[7:]:
        copy.wait()
    pushes = [gather.starts() for gather in gathers[1:]]

    t_at = lax.broadcasted_iota(jnp.int32, (slots, slots), 0)
    u_at = lax.broadcasted_iota(jnp.int32, (slots, slots), 1)
    for copy in locals_[3:6]:
        copy.wait()
    for i in range(gain_tiles.shape[0]):
        gain_ref[:, i * HEAD_SIZE:(i + 1) * HEAD_SIZE] = gain_tiles[i:i + 1, :]
    for s in range(samples):
        length = lens_ref[s]
        allowed = (u_at <= t_at) & ((u_at == t_at) | (mask_ref[s] == 1)) & (u_at < length)
        rows = pl.ds(own_rows + s * slots, slots)
        aux_buf[rows, 0:slots] = jnp.where(allowed, 1.0, 0.0).astype(jnp.bfloat16)
        aux_buf[rows, slots:2 * slots] = jnp.where(t_at < length, 1.0, 0.0).astype(jnp.bfloat16)
    send(aux_buf.at[pl.ds(own_rows, own_rows)], aux_buf.at[pl.ds(0, own_rows)], pair_recv.at[slabs], pair)

    def expand(group):
        for s in range(samples):
            at = slice(s * slots, (s + 1) * slots)
            rows = slice(group * own_rows + s * slots, group * own_rows + (s + 1) * slots)
            may_buf[rows, at] = aux_buf[rows, 0:slots].astype(jnp.float32)

    all_ctx = n_dev * ctx_rows

    def project_step(group):
        rows = pl.ds(group * own_rows, own_rows)
        keyval_buf[group, pl.ds(all_ctx, own_rows), :] = jnp.dot(
            rows_buf[rows, :], wkv_buf[...], preferred_element_type=jnp.float32
        ).astype(jnp.bfloat16)

    def project_query(i, first, count):
        rows = pl.ds(first, count)
        q = jnp.dot(rows_buf[rows, :], wq_bufs[i][...], preferred_element_type=jnp.float32)
        for h in range(widths[i]):
            q_buf[h, rows, :] = q[:, h * HEAD_SIZE:(h + 1) * HEAD_SIZE].astype(jnp.bfloat16)

    score_scale = 1.0 / math.sqrt(HEAD_SIZE)
    contract_last = (((1,), (1,)), ((), ()))
    firsts = [sum(widths[:i]) * HEAD_SIZE for i in range(groups)]

    def attend(i, group):
        heads = widths[i]
        rows = pl.ds(group * own_rows, own_rows)
        q = q_buf[0:heads, rows, :].reshape(heads * own_rows, HEAD_SIZE)
        scores = lax.dot_general(
            q, keyval_buf[group, :, 0:HEAD_SIZE], contract_last, preferred_element_type=jnp.float32
        ) * score_scale
        may = may_buf[rows, :] > 0.5
        step_scores = scores[:, all_ctx:].reshape(heads, own_rows, own_rows)
        step_scores = jnp.where(may[None], step_scores, NEG_FILL).reshape(heads * own_rows, own_rows)
        ctx_scores = scores[:, 0:all_ctx]
        top = jnp.maximum(
            jnp.max(ctx_scores, axis=-1, keepdims=True), jnp.max(step_scores, axis=-1, keepdims=True)
        )
        ctx_weights = jnp.exp(ctx_scores - top)
        step_weights = jnp.exp(step_scores - top)
        weight_sum = jnp.sum(ctx_weights, axis=-1, keepdims=True)
        weight_sum += jnp.sum(step_weights, axis=-1, keepdims=True)
        attended = jnp.dot(
            ctx_weights.astype(jnp.bfloat16), keyval_buf[group, pl.ds(0, all_ctx), HEAD_SIZE:],
            preferred_element_type=jnp.float32,
        )
        attended += jnp.dot(
            step_weights.astype(jnp.bfloat16), keyval_buf[group, pl.ds(all_ctx, own_rows), HEAD_SIZE:],
            preferred_element_type=jnp.float32,
        )
        attended = (attended / weight_sum).reshape(heads, own_rows, HEAD_SIZE)
        live = aux_buf[rows, slots:slots + 1].astype(jnp.float32) > 0.5
        attended = jnp.where(live[None], attended, 0.0).astype(jnp.bfloat16)
        for h in range(heads):
            col = firsts[i] + h * HEAD_SIZE
            if group == 0:
                part_buf[:, col:col + HEAD_SIZE] = attended[h]
            else:
                first = pl.multiple_of(head * half_cols + col, HEAD_SIZE)
                out_ref[:, pl.ds(first, HEAD_SIZE)] = attended[h]
        if group == 0:
            width = heads * HEAD_SIZE
            first = pl.multiple_of(head * half_cols + firsts[i], HEAD_SIZE)
            here = part_buf.at[:, pl.ds(firsts[i], width)]
            send(here, out_ref.at[:, pl.ds(first, width)], out_recv.at[i], pair)

    may_buf[...] = jnp.zeros_like(may_buf)
    expand(1)
    norm_rows(ctx_ref, ctx_buf, gain_ref, ctx_rows, 0)
    run(gathers[0].along_line(), pushes[1])
    locals_[2].wait()
    norm_rows(rows_buf, rows_buf, gain_ref, own_rows, own_rows)
    run(gathers[0].across_line(), gathers[1].along_line(), pushes[2])
    gathers[0].finish()
    own_ckv = jnp.dot(ctx_buf[...], wkv_buf[...], preferred_element_type=jnp.float32)
    ckv_buf[pl.ds(pl.multiple_of(d * ctx_rows, 16), ctx_rows), :] = own_ckv.astype(jnp.bfloat16)
    run(ctx_gather.starts())
    project_step(1)
    run(gathers[1].across_line(), ctx_gather.along_line(), gathers[2].along_line(), sum(pushes[3:], []))
    run(ctx_gather.across_line())
    ctx_gather.finish()
    for group in range(2):
        keyval_buf[group, pl.ds(0, all_ctx), :] = ckv_buf[...]

    gathers[1].finish()
    project_query(0, own_rows, own_rows)
    attend(0, 1)
    run(gathers[2].across_line(), gathers[3].along_line() if groups > 2 else [])
    for i in range(slabs):
        ref = rows_buf.at[pl.ds(i * SLAB, SLAB)]
        pltpu.make_async_copy(ref, ref, pair_recv.at[i]).wait()
    ref = aux_buf.at[pl.ds(0, own_rows)]
    pltpu.make_async_copy(ref, ref, pair_recv.at[slabs]).wait()
    norm_rows(rows_buf, rows_buf, gain_ref, own_rows, 0)
    expand(0)
    project_step(0)
    project_query(0, 0, own_rows)
    attend(0, 0)

    for i in range(1, groups):
        across_next = gathers[2 + i].across_line() if i + 1 < groups else []
        along_next = gathers[3 + i].along_line() if i + 2 < groups else []
        run(along_next)
        gathers[1 + i].finish()
        project_query(i, 0, 2 * own_rows)
        run(across_next[:2])
        attend(i, 0)
        run(across_next[2:])
        attend(i, 1)

    col = 0
    for i in range(groups):
        width = widths[i] * HEAD_SIZE
        here = out_ref.at[:, pl.ds(pl.multiple_of((1 - head) * half_cols + col, HEAD_SIZE), width)]
        pltpu.make_async_copy(here, here, out_recv.at[i]).wait()
        col += width
    for copy, cond in pending:
        if cond is None:
            copy.wait_send()
        else:
            pl.when(cond)(copy.wait_send)


def local(ctx_hidden, step_hidden, norm_gain, w_query, w_keyval, step_lengths, step_mask, n_dev):
    samples, slots, features = step_hidden.shape
    own_rows = samples * slots
    query_cols = w_query.shape[1]
    widths = split_heads(query_cols // HEAD_SIZE // KEYVAL_HEADS)
    groups = len(widths)
    ctx_rows = ctx_hidden.shape[0]
    bf16 = jnp.bfloat16
    sends = (groups + 2) * (2 * n_dev) + own_rows // SLAB + 1 + groups
    vmem = pl.BlockSpec(memory_space=pltpu.VMEM)
    smem = pl.BlockSpec(memory_space=pltpu.SMEM)
    anywhere = pl.BlockSpec(memory_space=pl.ANY)
    out = pl.pallas_call(
        functools.partial(kernel, n_dev, samples, slots, widths),
        out_shape=jax.ShapeDtypeStruct((own_rows, query_cols), bf16),
        in_specs=[anywhere] * 5 + [smem, anywhere],
        out_specs=vmem,
        scratch_shapes=[
            pltpu.VMEM((ctx_rows, features), bf16),
            pltpu.VMEM((features // HEAD_SIZE, HEAD_SIZE), jnp.float32),
            pltpu.VMEM((1, features), jnp.float32),
            pltpu.VMEM((samples, slots, slots), jnp.int32),
            pltpu.VMEM((2 * own_rows, features), bf16),
            pltpu.VMEM((ctx_rows, features), bf16),
            pltpu.VMEM((features, 2 * HEAD_SIZE), bf16),
        ]
        + [pltpu.VMEM((features, width * HEAD_SIZE), bf16) for width in widths]
        + [
            pltpu.VMEM((n_dev * ctx_rows, 2 * HEAD_SIZE), bf16),
            pltpu.VMEM((2, n_dev * ctx_rows + own_rows, 2 * HEAD_SIZE), bf16),
            pltpu.VMEM((max(widths), 2 * own_rows, HEAD_SIZE), bf16),
            pltpu.VMEM((2 * own_rows, 2 * slots), bf16),
            pltpu.VMEM((2 * own_rows, own_rows), jnp.float32),
            pltpu.VMEM((own_rows, query_cols // 2), bf16),
            pltpu.SemaphoreType.DMA((groups + 2, 2, n_dev)),
            pltpu.SemaphoreType.DMA((sends,)),
            pltpu.SemaphoreType.DMA((6 + groups,)),
            pltpu.SemaphoreType.DMA((own_rows // SLAB + 1,)),
            pltpu.SemaphoreType.DMA((groups,)),
        ],
        compiler_params=pltpu.CompilerParams(
            collective_id=0, has_side_effects=True, vmem_limit_bytes=62 * 1024 * 1024
        ),
        name="shared_context_attention",
    )(
        ctx_hidden, step_hidden.reshape(own_rows, features), norm_gain.reshape(features // HEAD_SIZE, HEAD_SIZE),
        w_query, w_keyval, step_lengths, step_mask,
    )
    return out.reshape(samples, slots, query_cols)


def solution(mesh):
    placed = (
        P("dev", None),
        P(("grp", "dev"), None, None),
        P(),
        P("dev", None),
        P("dev", None),
        P(("grp", "dev")),
        P(("grp", "dev"), None, None),
    )
    return jax.shard_map(
        functools.partial(local, n_dev=mesh.shape["dev"]),
        mesh=mesh, in_specs=placed, out_specs=P(("grp", "dev"), None, None), check_vma=False,
    )
```
